512 devices in a mesh: gx: 16 (over x, y_hi), yz: 32 (over y_lo, z, core).
Axes of the slice: x: 4, y: 8 (y_hi: 4, y_lo: 2; y = y_hi * 2 + y_lo), z: 8, core: 2. Of those that a mesh axis runs over, the one named last changes fastest.
Arguments:
- tokens: bfloat16 [2048, 4096], P('gx', 'yz'), may hold values from -6 to 6
- gate_weight: bfloat16 [4096, 14336], P('gx', 'yz'), may hold values from -0.09375 to 0.09375
- up_weight: bfloat16 [4096, 14336], P('gx', 'yz'), may hold values from -0.09375 to 0.09375
- down_weight: bfloat16 [14336, 4096], P('yz', 'gx'), may hold values from -0.046875 to 0.046875
- decode_in: bfloat16 [4, 96, 4096], P(None, 'gx'), may hold values from -6 to 6
Outputs:
- prefill_out: bfloat16 [2048, 4096], P(('gx', 'yz'))
- decode_out: bfloat16 [4, 96, 4096], P(None, 'yz', 'gx')
The draws below stay inside these ranges and needn't reach their ends.
All inputs are finite; a program needn't handle non-finite values.
Results may differ from the reference program's by a relative error of at most 0.0049.
Values may be sent and summed in bfloat16 or wider, within the bound.
No kernel may reach another device: no remote copies, remote signals or barrier semaphores. Data moves between devices by JAX's collectives and lax.ppermute only.
A program may use at most 64 MiB of HBM per device.

```python
import jax
import jax.numpy as jnp

D = 4096
FF = 14336
STEPS = 4
TOKENS = 2048
DEC_ROWS = 96


def level_of(rng, shape, split, least, high):
    def one(dim, blocks):
        heights = jax.random.uniform(jax.random.fold_in(jax.random.fold_in(rng, 6), dim), (blocks,), jnp.float32, least / len(split), high / len(split))
        return jnp.repeat(jnp.exp(heights), shape[dim] // blocks).reshape((-1,) + (1,) * (len(shape) - dim - 1))

    loudness = one(*split[0])
    for cut in split[1:]:
        loudness = loudness * one(*cut)
    return loudness


def noise(key, shape, scale, limit, pieces=(), held_as=jnp.bfloat16):
    factor_of = level_of(key, shape, pieces, -0.22, 0.18) if pieces else 1.0
    drawn = jax.random.normal(key, shape, jnp.float32) * scale * factor_of
    return jnp.minimum(jnp.maximum(drawn, -limit), limit).astype(held_as)


def setup_inputs(seed: int = 0) -> dict:
    arg_keys = jax.random.split(jax.random.key(seed), 6)
    return {
        "tokens": noise(arg_keys[0], (TOKENS, D), 1.0, 6.0, ((0, 16), (1, 32))),
        "gate_weight": noise(arg_keys[1], (D, FF), D ** -0.5, 0.09375, ((0, 16), (1, 32))),
        "up_weight": noise(arg_keys[2], (D, FF), D ** -0.5, 0.09375, ((0, 16), (1, 32))),
        "down_weight": noise(arg_keys[3], (FF, D), FF ** -0.5, 0.046875, ((0, 32), (1, 16))),
        "decode_in": noise(arg_keys[4], (STEPS, DEC_ROWS, D), 1.0, 6.0, ((1, 16),)),
    }


def layer_rows(inputs, gate_weight, up_weight, down_weight):
    gate_part = jnp.dot(inputs, gate_weight, preferred_element_type=jnp.float32)
    up_part = jnp.dot(inputs, up_weight, preferred_element_type=jnp.float32)
    hidden = (jax.nn.silu(gate_part) * up_part).astype(jnp.bfloat16)
    return jnp.dot(hidden, down_weight, preferred_element_type=jnp.float32).astype(jnp.bfloat16)


def reference(tokens, gate_weight, up_weight, down_weight, decode_in):
    prefill_out = layer_rows(tokens, gate_weight, up_weight, down_weight)
    results = []
    for step in range(STEPS):
        results.append(layer_rows(decode_in[step], gate_weight, up_weight, down_weight))
    decode_out = jnp.stack(results)
    return (prefill_out, decode_out)
```

```python
import jax
import jax.numpy as jnp
from jax import lax
from jax.sharding import Mesh, PartitionSpec as P

BF16 = jnp.bfloat16
F32 = jnp.float32
SIZES = (("x", 4), ("h", 4), ("l", 2), ("a", 2), ("b", 4), ("c", 2))
GX = ("x", "h")
LZ = ("l", "a", "b")


def swap_cores(value):
    return lax.ppermute(value, "c", [(0, 1), (1, 0)])


def exchange(blocks, axes):
    return lax.all_to_all(blocks, axes, split_axis=0, concat_axis=0, tiled=True)


def local(tokens, gate_weight, up_weight, down_weight, decode_in):
    core = lax.axis_index("c")
    yz = lax.axis_index(("l", "a", "b", "c"))
    steps, rows, width = decode_in.shape
    ff = gate_weight.shape[1]
    n_rows = tokens.shape[0]
    n_dec = steps * rows
    block = tokens.shape[1]

    halves = down_weight.reshape(ff, 2, block)
    kept = lax.dynamic_index_in_dim(halves, core, 1, keepdims=False)
    given = lax.dynamic_index_in_dim(halves, 1 - core, 1, keepdims=False)
    taken = swap_cores(given)
    both = jnp.where(core == 0, jnp.stack([kept, taken]), jnp.stack([taken, kept]))
    gate_up = jnp.concatenate([gate_weight, up_weight], axis=1)
    gate_up = lax.all_gather(gate_up, "x", axis=0, tiled=True)
    down = lax.all_gather(both.reshape(2 * ff, block), GX, axis=0, tiled=False)

    decode_part = lax.dynamic_slice_in_dim(decode_in.reshape(n_dec, width), yz * block, block, 1)
    feats = jnp.concatenate([tokens, decode_part], axis=0)
    feats = lax.ppermute(
        feats, ("h", "b"), [(h * 4 + b, b * 4 + h) for h in range(4) for b in range(4)]
    )
    total = n_rows + n_dec
    feats = exchange(jnp.broadcast_to(feats, (16, total, block)), LZ)
    other = swap_cores(feats)
    pair = jnp.where(core == 0, jnp.stack([feats, other]), jnp.stack([other, feats]))
    feats = pair.reshape(2, 4, 4, total, block).transpose(2, 3, 1, 0, 4).reshape(4 * total, -1)

    partial = jnp.dot(feats, gate_up, preferred_element_type=F32).astype(BF16)
    sums = exchange(partial.reshape(4, total, 2 * ff), "h").astype(F32).sum(0)
    hidden = (jax.nn.silu(sums[:, :ff]) * sums[:, ff:]).astype(BF16)

    other = swap_cores(hidden)
    hidden = jnp.where(
        core == 0,
        jnp.concatenate([hidden, other], axis=1),
        jnp.concatenate([other, hidden], axis=1),
    )
    out = jnp.einsum("rk,gkn->rgn", hidden, down, preferred_element_type=F32).astype(BF16)
    prefill = out[:n_rows].reshape(16, n_rows, block)
    decode = out[n_rows:].transpose(1, 0, 2)
    sums = exchange(jnp.concatenate([prefill, decode], axis=1), LZ).astype(F32).sum(0).astype(BF16)

    prefill = sums[:n_rows].reshape(2, n_rows // 2, block)
    decode = sums[n_rows:].reshape(steps, 2, rows // 2, block).transpose(1, 0, 2, 3)
    decode = decode.reshape(2, n_dec // 2, block)
    mine = jnp.concatenate([prefill, decode], axis=1)
    kept = lax.dynamic_index_in_dim(mine, core, 0, keepdims=False)
    given = lax.dynamic_index_in_dim(mine, 1 - core, 0, keepdims=False)
    taken = swap_cores(given)
    joined = jnp.where(
        core == 0,
        jnp.concatenate([kept, taken], axis=1),
        jnp.concatenate([taken, kept], axis=1),
    )
    prefill_out = joined[: n_rows // 2].reshape(n_rows // 32, 16 * 2 * block)
    decode = joined[n_rows // 2 :]
    decode = lax.ppermute(
        decode,
        ("x", "h", "l", "a", "b"),
        [(g * 16 + y, y * 16 + g) for g in range(16) for y in range(16)],
    )
    decode_out = decode.reshape(steps, rows // 2, 2 * block)
    return prefill_out, decode_out


def solution(mesh):
    sizes = [size for _, size in SIZES]
    fine = Mesh(mesh.devices.reshape(sizes), [name for name, _ in SIZES])
    gx, yz = GX, ("l", "a", "b", "c")
    return jax.shard_map(
        local,
        mesh=fine,
        in_specs=(P(gx, yz), P(gx, yz), P(gx, yz), P(yz, gx), P(None, gx, None)),
        out_specs=(P(gx + yz, None), P(None, yz, gx)),
        check_vma=False,
    )
```

```python
import jax
import jax.numpy as jnp
from jax import lax
from jax.experimental import pallas as pl
from jax.experimental.pallas import tpu as pltpu
from jax.sharding import Mesh, PartitionSpec as P

BF16 = jnp.bfloat16
F32 = jnp.float32
SIZES = (("x", 4), ("h", 4), ("l", 2), ("a", 2), ("b", 4), ("c", 2))
GX = ("x", "h")
LZ = ("l", "a", "b")
UP = [(i, (i + 1) % 4) for i in range(4)]
DOWN = [(i, (i + 3) % 4) for i in range(4)]
VMEM = 16 * 2**20
HINTS = (20, 3)


def swap_cores(value):
    return lax.ppermute(value, "c", [(0, 1), (1, 0)])


def exchange(blocks, axes):
    return lax.all_to_all(blocks, axes, split_axis=0, concat_axis=0, tiled=True)


def near(value, axis):
    return lax.ppermute(value, axis, DOWN), lax.ppermute(value, axis, UP)


def far(following, previous, axis, hint):
    shape = previous.shape[:-2] + (previous.shape[-2] // 2, previous.shape[-1])
    halves = jax.ShapeDtypeStruct(shape, BF16)
    up, down = call(halves_kernel, (halves, halves), hint)(previous, following)
    return lax.ppermute(up, axis, UP), lax.ppermute(down, axis, DOWN)


def call(kernel, outs, hint, scratch=()):
    return pl.pallas_call(
        kernel,
        out_shape=outs,
        scratch_shapes=list(scratch),
        compiler_params=pltpu.CompilerParams(vmem_limit_bytes=VMEM),
        cost_estimate=pl.CostEstimate(flops=int(hint * 1.1e9), bytes_accessed=2**20, transcendentals=0),
    )


def dot(lhs, rhs):
    return jnp.dot(lhs, rhs, preferred_element_type=F32)


def weights_kernel(gate, up, down, out):
    depth, ff = gate.shape
    whole = ff // 128
    for k in range(whole):
        out[k * depth : (k + 1) * depth] = gate[:, k * 128 : (k + 1) * 128]
        out[(whole + k) * depth : (whole + k + 1) * depth] = up[:, k * 128 : (k + 1) * 128]
    out[2 * whole * depth : (2 * whole + 1) * depth] = jnp.concatenate(
        [gate[:, whole * 128 :], up[:, whole * 128 :]], axis=1
    )
    base = (2 * whole + 1) * depth
    for k in range(down.shape[1] // 128):
        out[base + k * ff : base + (k + 1) * ff] = down[:, k * 128 : (k + 1) * 128]


def halves_kernel(previous, following, up, down):
    half = up.shape[-2]
    up[...] = previous[..., :half, :]
    down[...] = following[..., half:, :]


def gate_up_kernel(mine, other, own, following, first, second, previous, partial, kept, opposite):
    x, h, core = lax.axis_index("x"), lax.axis_index("h"), lax.axis_index("c")
    half = first.shape[0]
    depth = 2 * mine.shape[2]
    tiles = partial.shape[2] // 128
    opposite[:half] = first[...]
    opposite[half:] = second[...]

    def rows(b, carry):
        total = None
        for slot, weight in enumerate((own, following, opposite, previous)):
            at = lax.rem(x + slot, 4) * 4 + b
            left = jnp.where(core == 0, mine[at], other[at])
            right = jnp.where(core == 0, other[at], mine[at])
            wide = jnp.concatenate([weight[k * depth : (k + 1) * depth] for k in range(tiles)], axis=1)
            term = dot(jnp.concatenate([left, right], axis=1), wide)
            total = term if total is None else total + term
        partial[b] = total.astype(BF16)

        @pl.when(b == h)
        def _():
            kept[...] = total

        return carry

    lax.fori_loop(0, 4, rows, 0)


def hidden_kernel(parts, own_part, out):
    h = lax.axis_index("h")
    copies, _, ff = out.shape
    sums = own_part[...]
    for source in range(4):
        part = parts[source].astype(F32)
        sums = sums + jnp.where(source == h, jnp.zeros_like(part), part)
    even = ff // 128 * 128
    gate, up, tail = sums[:, :even], sums[:, even : 2 * even], sums[:, 2 * even :]
    wide = (gate / (1.0 + jnp.exp(-gate)) * up).astype(BF16)
    gate, up = tail[:, : ff - even], tail[:, ff - even :]
    last = (gate / (1.0 + jnp.exp(-gate)) * up).astype(BF16)
    for k in range(copies):
        out[k, :, :even] = wide
        out[k, :, even:] = last


def down_kernel(hidden, own, following, second, previous, kept, given):
    x, core = lax.axis_index("x"), lax.axis_index("c")
    blocks, rows, ff = hidden.shape
    half = rows // 2
    tiles = kept.shape[2] // 128
    mine = pl.ds(pl.multiple_of(core * half, 16), half)
    other = pl.ds(pl.multiple_of((1 - core) * half, 16), half)
    lhs = jnp.concatenate([hidden[k, part] for part in (mine, other) for k in range(blocks)], axis=0)
    for slot, weight in enumerate((own, following, second, previous)):
        base = weight.shape[0] - tiles * ff
        wide = jnp.concatenate([weight[base + t * ff : base + (t + 1) * ff] for t in range(tiles)], axis=1)
        terms = dot(lhs, wide)
        at = lax.rem(x + slot, 4) * blocks
        for k in range(blocks):
            kept[at + k] = terms[k * half : (k + 1) * half]
            given[at + k] = terms[(blocks + k) * half : (blocks + k + 1) * half].astype(BF16)


def local(tokens, gate_weight, up_weight, down_weight, decode_in):
    yz = lax.axis_index(("l", "a", "b", "c"))
    steps, rows, _ = decode_in.shape
    depth, ff = gate_weight.shape
    n_rows, block = tokens.shape
    n_dec = steps * rows
    width = down_weight.shape[1]
    each = -(-(n_rows + n_dec) // 32) * 16
    total = 2 * each
    fill = each - (n_rows + n_dec) // 2

    decode_part = lax.dynamic_slice_in_dim(decode_in, yz * block, block, 2)
    feats = jnp.concatenate(
        [
            tokens.reshape(16, 2, 4, block).transpose(1, 0, 2, 3).reshape(2, n_rows // 2, block),
            decode_part.reshape(steps, 2, rows // 2, block).transpose(1, 0, 2, 3).reshape(2, n_dec // 2, block),
            jnp.zeros((2, fill, block), BF16),
        ],
        axis=1,
    ).reshape(total, block)
    feats = lax.ppermute(
        feats, ("h", "b"), [(h * 4 + b, b * 4 + h) for h in range(4) for b in range(4)]
    )
    feats = exchange(jnp.broadcast_to(feats, (16, total, block)), LZ)
    pieces = (2 * ff // 128 * depth + width // 128 * ff, 128)
    own = call(weights_kernel, jax.ShapeDtypeStruct(pieces, BF16), 1)(gate_weight, up_weight, down_weight)
    own_near = near(own, "x")
    own_far = far(*own_near, "x", HINTS[0])
    other = swap_cores(feats)

    partial, kept = call(
        gate_up_kernel,
        (
            jax.ShapeDtypeStruct((4, total, 2 * ff), BF16),
            jax.ShapeDtypeStruct((total, 2 * ff), F32),
        ),
        HINTS[1],
        [pltpu.VMEM(pieces, BF16)],
    )(feats, other, own, own_near[0], *own_far, own_near[1])
    parts = exchange(partial, "h")
    hidden = call(hidden_kernel, jax.ShapeDtypeStruct((4, total, ff), BF16), 2)(parts, kept)
    hidden = exchange(hidden, "h")
    kept, given = call(
        down_kernel,
        (
            jax.ShapeDtypeStruct((16, each, width), F32),
            jax.ShapeDtypeStruct((16, each, width), BF16),
        ),
        2,
    )(hidden, own, own_near[0], own_far[1], own_near[1])
    sums = (kept + swap_cores(given).astype(F32)).astype(BF16)

    half = n_rows // 2
    prefill = sums[:, :half].reshape(16, 16, 4, width).transpose(1, 0, 2, 3).reshape(16, half, width)
    sums = exchange(jnp.concatenate([prefill, sums[:, half:]], axis=1), LZ)
    sums = sums.astype(F32).sum(0).astype(BF16)
    decode_out = lax.ppermute(
        sums[half : half + n_dec // 2],
        ("x", "l", "a"),
        [(i * 4 + j, j * 4 + i) for i in range(4) for j in range(4)],
    ).reshape(steps, rows // 2, width)
    prefill_out = exchange(sums[:half].reshape(4, 4, 4, width).transpose(1, 0, 2, 3), "h")
    prefill_out = prefill_out.transpose(2, 1, 0, 3).reshape(4, 16 * width)
    return prefill_out, decode_out


def solution(mesh):
    sizes = [size for _, size in SIZES]
    fine = Mesh(mesh.devices.reshape(sizes), [name for name, _ in SIZES])
    gx, yz = GX, ("l", "a", "b", "c")
    return jax.shard_map(
        local,
        mesh=fine,
        in_specs=(P(gx, yz), P(gx, yz), P(gx, yz), P(yz, gx), P(None, gx, None)),
        out_specs=(P(gx + yz, None), P(None, yz, gx)),
        check_vma=False,
    )
```

```python
import jax
import jax.numpy as jnp
from jax import lax
from jax.experimental import pallas as pl
from jax.experimental.pallas import tpu as pltpu
from jax.sharding import Mesh, PartitionSpec as P

BF16 = jnp.bfloat16
F32 = jnp.float32
SIZES = (("x", 4), ("h", 4), ("l", 2), ("a", 2), ("b", 4), ("c", 2))
GX = ("x", "h")
LZ = ("l", "a", "b")
UP = [(i, (i + 1) % 4) for i in range(4)]
DOWN = [(i, (i + 3) % 4) for i in range(4)]
VMEM = 16 * 2**20
HINTS = (5.5, 0.1, 1, 8, 5)


def swap_cores(value):
    return lax.ppermute(value, "c", [(0, 1), (1, 0)])


def exchange(blocks, axes):
    return lax.all_to_all(blocks, axes, split_axis=0, concat_axis=0, tiled=True)


def near(value, axis):
    return lax.ppermute(value, axis, DOWN), lax.ppermute(value, axis, UP)


def far(following, previous, axis, hint):
    shape = previous.shape[:-2] + (previous.shape[-2] // 2, previous.shape[-1])
    halves = jax.ShapeDtypeStruct(shape, BF16)
    up, down = call(halves_kernel, (halves, halves), hint)(previous, following)
    return lax.ppermute(up, axis, UP), lax.ppermute(down, axis, DOWN)


def call(kernel, outs, hint, scratch=(), vmem=VMEM, **more):
    return pl.pallas_call(
        kernel,
        out_shape=outs,
        scratch_shapes=list(scratch),
        compiler_params=pltpu.CompilerParams(vmem_limit_bytes=vmem),
        cost_estimate=pl.CostEstimate(flops=int(hint * 1.1e9), bytes_accessed=2**20, transcendentals=0),
        **more,
    )


def dot(lhs, rhs):
    return jnp.dot(lhs, rhs, preferred_element_type=F32)


def weights_kernel(gate, up, out):
    ff = gate.shape[0]
    even = ff // 128 * 128
    out[:even] = gate[:even]
    out[even : 2 * even] = up[:even]
    out[2 * even : even + ff] = gate[even:]
    out[even + ff :] = up[even:]


def halves_kernel(previous, following, up, down):
    half = up.shape[-2]
    up[...] = previous[..., :half, :]
    down[...] = following[..., half:, :]


def pair_kernel(own, opposite, out):
    out[0] = own[...]
    out[1] = opposite[...]


def gate_up_kernel(mine, other, own, following, first, second, previous, partial, residue):
    x, h, core = lax.axis_index("x"), lax.axis_index("h"), lax.axis_index("c")
    blocks, rows, _ = partial.shape
    opposite = jnp.concatenate([first[...], second[...]], axis=0)
    total = None
    for slot, weight in enumerate((own[...], following[...], opposite, previous[...])):
        lhs = []
        for b in range(blocks):
            at = lax.rem(x + slot, 4) * 4 + b
            left = jnp.where(core == 0, mine[at], other[at])
            right = jnp.where(core == 0, other[at], mine[at])
            lhs.append(jnp.concatenate([left, right], axis=1))
        term = lax.dot_general(
            jnp.concatenate(lhs, axis=0), weight, (((1,), (1,)), ((), ())), preferred_element_type=F32
        )
        total = term if total is None else total + term
    for b in range(blocks):
        part = total[b * rows : (b + 1) * rows]
        rounded = part.astype(BF16)
        partial[b] = rounded

        @pl.when(b == h)
        def _():
            residue[...] = (part - rounded.astype(F32)).astype(BF16)


def hidden_kernel(parts, residue, out):
    ff = out.shape[1]
    sums = residue[...].astype(F32)
    for source in range(4):
        sums = sums + parts[source].astype(F32)
    even = ff // 128 * 128
    gate, up, tail = sums[:, :even], sums[:, even : 2 * even], sums[:, 2 * even :]
    out[:, :even] = (gate / (1.0 + jnp.exp(-gate)) * up).astype(BF16)
    gate, up = tail[:, : ff - even], tail[:, ff - even :]
    out[:, even:] = (gate / (1.0 + jnp.exp(-gate)) * up).astype(BF16)


def down_kernel(hidden, partner, own, following, first, second, previous, kept, given):
    x, core = lax.axis_index("x"), lax.axis_index("c")
    half = hidden.shape[0] // 2
    mine = pl.ds(pl.multiple_of(core * half, 16), half)
    other = pl.ds(pl.multiple_of((1 - core) * half, 16), half)
    lhs = jnp.concatenate([ref[part] for part in (mine, other) for ref in (hidden, partner)], axis=0)
    for slot in range(4):
        for k in range(2):
            if slot == 2:
                weight = jnp.concatenate([first[k], second[k]], axis=0)
            else:
                weight = (own, following, None, previous)[slot][k]
            terms = dot(lhs, weight)
            at = lax.rem(x + slot, 4) * 4 + k * 2
            for r in range(2):
                kept[at + r] = terms[r * half : (r + 1) * half]
                given[at + r] = terms[(2 + r) * half : (3 + r) * half].astype(BF16)


def decode_kernel(rows, out):
    steps = out.shape[1]
    wide = rows[...].astype(F32)
    for i in range(out.shape[0]):
        out[i] = wide[i * steps : (i + 1) * steps].astype(BF16)


def local(tokens, gate_weight, up_weight, down_weight, decode_in):
    yz = lax.axis_index(("l", "a", "b", "c"))
    steps, rows, _ = decode_in.shape
    depth, ff = gate_weight.shape
    n_rows, block = tokens.shape
    n_dec = steps * rows
    width = down_weight.shape[1]
    each = -(-(n_rows + n_dec) // 32) * 16
    total = 2 * each
    fill = each - (n_rows + n_dec) // 2

    decode_part = lax.dynamic_slice_in_dim(decode_in, yz * block, block, 2)
    feats = jnp.concatenate(
        [
            tokens.reshape(16, 2, 4, block).transpose(1, 0, 2, 3).reshape(2, n_rows // 2, block),
            decode_part.transpose(1, 0, 2).reshape(2, n_dec // 2, block),
            jnp.zeros((2, fill, block), BF16),
        ],
        axis=1,
    ).reshape(total, block)
    feats = lax.ppermute(
        feats, ("h", "b"), [(h * 4 + b, b * 4 + h) for h in range(4) for b in range(4)]
    )
    feats = exchange(jnp.broadcast_to(feats, (16, total, block)), LZ)
    own = call(weights_kernel, jax.ShapeDtypeStruct((2 * ff, depth), BF16), 1)(
        gate_weight.T, up_weight.T
    )
    own_near = near(own, "x")
    own_far = far(*own_near, "x", HINTS[0])
    opposite = lax.ppermute(down_weight, "h", [(i, (i + 2) % 4) for i in range(4)])
    feats, own_far = lax.optimization_barrier((feats, own_far))
    other = swap_cores(feats)
    down = call(pair_kernel, jax.ShapeDtypeStruct((2, ff, width), BF16), HINTS[3])(down_weight, opposite)
    other, down = lax.optimization_barrier((other, down))

    partial, residue = call(
        gate_up_kernel,
        (
            jax.ShapeDtypeStruct((4, total, 2 * ff), BF16),
            jax.ShapeDtypeStruct((total, 2 * ff), BF16),
        ),
        HINTS[1],
    )(feats, other, own, own_near[0], *own_far, own_near[1])
    parts = exchange(partial, "h")
    hidden = call(hidden_kernel, jax.ShapeDtypeStruct((total, ff), BF16), 1)(parts, residue)
    beside = [(0, 1), (1, 0), (2, 3), (3, 2)]
    partner = lax.ppermute(hidden, "h", beside)
    down_near = near(down, "x")
    down_far = far(*down_near, "x", HINTS[2])
    kept, given = call(
        down_kernel,
        (
            jax.ShapeDtypeStruct((16, each, width), F32),
            jax.ShapeDtypeStruct((16, each, width), BF16),
        ),
        2,
    )(hidden, partner, down, down_near[0], *down_far, down_near[1])
    sums = (kept + swap_cores(given).astype(F32)).astype(BF16)

    half = n_rows // 2
    prefill = sums[:, :half].reshape(16, 16, 4, width).transpose(1, 0, 2, 3).reshape(16, half, width)
    sums = exchange(jnp.concatenate([prefill, sums[:, half:]], axis=1), LZ)
    sums = sums.astype(F32).sum(0).astype(BF16)
    decode_out = lax.ppermute(
        sums[half : half + n_dec // 2],
        ("x", "h", "l", "a", "b"),
        [
            (
                x * 64 + h * 16 + q * 4 + k * 2 + r,
                q * 64 + (h ^ 2 * k) * 16 + x * 4 + (h ^ r),
            )
            for x in range(4)
            for h in range(4)
            for q in range(4)
            for k in range(2)
            for r in range(2)
        ],
    )
    decode_out = call(decode_kernel, jax.ShapeDtypeStruct((rows // 2, steps, width), BF16), HINTS[4])(decode_out)
    decode_out = decode_out.transpose(1, 0, 2)
    h = lax.axis_index("h")
    mine = sums[:half].reshape(4, 2, 2, 4, width)
    theirs = lax.ppermute(mine[:, :, 1], "h", beside)
    both = jnp.stack([mine[:, :, 0], theirs], axis=2)
    both = jnp.where(h % 2 == 1, both[:, :, ::-1], both)
    both = jnp.where(h // 2 == 1, both[:, ::-1], both)
    prefill_out = both.transpose(3, 0, 1, 2, 4).reshape(4, 16 * width)
    return prefill_out, decode_out


def solution(mesh):
    sizes = [size for _, size in SIZES]
    fine = Mesh(mesh.devices.reshape(sizes), [name for name, _ in SIZES])
    gx, yz = GX, ("l", "a", "b", "c")
    return jax.shard_map(
        local,
        mesh=fine,
        in_specs=(P(gx, yz), P(gx, yz), P(gx, yz), P(yz, gx), P(None, gx, None)),
        out_specs=(P(gx + yz, None), P(None, yz, gx)),
        check_vma=False,
    )
```

```python
import jax
import jax.numpy as jnp
from jax import lax
from jax.experimental import pallas as pl
from jax.experimental.pallas import tpu as pltpu
from jax.sharding import Mesh, PartitionSpec as P

BF16 = jnp.bfloat16
F32 = jnp.float32
SIZES = (("x", 4), ("h", 4), ("l", 2), ("a", 2), ("b", 4), ("c", 2))
GX = ("x", "h")
LZ = ("l", "a", "b")
UP = [(i, (i + 1) % 4) for i in range(4)]
DOWN = [(i, (i + 3) % 4) for i in range(4)]
VMEM = 16 * 2**20
HINTS = (5.5, 0.1, 1, 0.1, 5, 8, 5)


def swap_cores(value):
    return lax.ppermute(value, "c", [(0, 1), (1, 0)])


def exchange(blocks, axes):
    return lax.all_to_all(blocks, axes, split_axis=0, concat_axis=0, tiled=True)


def near(value, axis):
    return lax.ppermute(value, axis, DOWN), lax.ppermute(value, axis, UP)


def far(following, previous, axis, hint):
    shape = previous.shape[:-2] + (previous.shape[-2] // 2, previous.shape[-1])
    halves = jax.ShapeDtypeStruct(shape, BF16)
    up, down = call(halves_kernel, (halves, halves), hint)(previous, following)
    return lax.ppermute(up, axis, UP), lax.ppermute(down, axis, DOWN)


def call(kernel, outs, hint, scratch=(), vmem=VMEM, **more):
    return pl.pallas_call(
        kernel,
        out_shape=outs,
        scratch_shapes=list(scratch),
        compiler_params=pltpu.CompilerParams(vmem_limit_bytes=vmem),
        cost_estimate=pl.CostEstimate(flops=int(hint * 1.1e9), bytes_accessed=2**20, transcendentals=0),
        **more,
    )


def dot(lhs, rhs):
    return jnp.dot(lhs, rhs, preferred_element_type=F32)


def weights_kernel(gate, up, out):
    ff = gate.shape[0]
    even = ff // 128 * 128
    out[:even] = gate[:even]
    out[even : 2 * even] = up[:even]
    out[2 * even : even + ff] = gate[even:]
    out[even + ff :] = up[even:]


def halves_kernel(previous, following, up, down):
    half = up.shape[-2]
    up[...] = previous[..., :half, :]
    down[...] = following[..., half:, :]


def pair_kernel(own, opposite, out):
    out[0] = own[...]
    out[1] = opposite[...]


def half_product(feats, weights, which):
    x = lax.axis_index("x")
    own, following, first, second, previous = weights
    block = feats.shape[2]
    part = pl.ds(pl.multiple_of(which * block, block), block)
    opposite = jnp.concatenate([first[:, part], second[:, part]], axis=0)
    total = None
    for slot, weight in enumerate((own[:, part], following[:, part], opposite, previous[:, part])):
        lhs = jnp.concatenate([feats[lax.rem(x + slot, 4) * 4 + b] for b in range(4)], axis=0)
        term = lax.dot_general(lhs, weight, (((1,), (1,)), ((), ())), preferred_element_type=F32)
        total = term if total is None else total + term
    return total


def gate_up_start_kernel(feats, own, following, first, second, previous, out):
    out[...] = half_product(feats, (own, following, first, second, previous), lax.axis_index("c"))


def gate_up_kernel(feats, started, own, following, first, second, previous, partial, residue):
    h = lax.axis_index("h")
    blocks, rows, _ = partial.shape
    stride = feats.shape[1]
    weights = (own, following, first, second, previous)
    total = started[...] + half_product(feats, weights, 1 - lax.axis_index("c"))
    for b in range(blocks):
        part = total[b * stride : b * stride + rows]
        rounded = part.astype(BF16)
        partial[b] = rounded

        @pl.when(b == h)
        def _():
            residue[...] = (part - rounded.astype(F32)).astype(BF16)


def hidden_kernel(parts, residue, out):
    ff = out.shape[1]
    sums = residue[...].astype(F32)
    for source in range(4):
        sums = sums + parts[source].astype(F32)
    even = ff // 128 * 128
    gate, up, tail = sums[:, :even], sums[:, even : 2 * even], sums[:, 2 * even :]
    out[:, :even] = (gate / (1.0 + jnp.exp(-gate)) * up).astype(BF16)
    gate, up = tail[:, : ff - even], tail[:, ff - even :]
    out[:, even:] = (gate / (1.0 + jnp.exp(-gate)) * up).astype(BF16)


def down_products(half, hidden, own, following, first, second, previous, store):
    x, core = lax.axis_index("x"), lax.axis_index("c")
    mine = hidden[pl.ds(pl.multiple_of(core * half, 16), half)]
    other = hidden[pl.ds(pl.multiple_of((1 - core) * half, 16), half)]
    decode = hidden[2 * half :].astype(F32)
    low, high = decode[:16].astype(BF16), decode[8:].astype(BF16)
    lhs = jnp.concatenate(
        [mine, jnp.where(core == 0, low, high), other, jnp.where(core == 0, high, low)], axis=0
    )
    for slot in range(4):
        for k in range(2):
            if slot == 2:
                weight = jnp.concatenate([first[k], second[k]], axis=0)
            else:
                weight = (own, following, None, previous)[slot][k]
            terms = dot(lhs, weight)
            store(lax.rem(x + slot, 4) * 2 + k, terms[: half + 16], terms[half + 16 :].astype(BF16))


def down_start_kernel(hidden, own, following, first, second, previous, kept, given):
    def store(at, mine, other):
        kept[at] = mine
        given[at] = other

    down_products(kept.shape[1] - 16, hidden, own, following, first, second, previous, store)


def down_kernel(hidden, own, following, first, second, previous, kept0, given0, kept, given):
    def store(at, mine, other):
        kept[at, 1] = mine
        given[at, 1] = other

    down_products(kept.shape[2] - 16, hidden, own, following, first, second, previous, store)
    kept[:, 0] = kept0[...]
    given[:, 0] = given0[...]


def prefill_kernel(mine, theirs, out):
    h = lax.axis_index("h")
    width = mine.shape[3]
    for q in range(mine.shape[0]):
        for k in range(mine.shape[1]):
            column = lax.bitwise_xor(h, 2 * k)
            for ref, at in ((mine, column), (theirs, lax.bitwise_xor(column, 1))):
                out[:, pl.ds(pl.multiple_of((q * 4 + at) * width, width), width)] = ref[q, k]


def decode_kernel(rows, out):
    core = lax.axis_index("c")
    count, steps, _ = out.shape
    wide = rows[...].astype(F32)
    skip = wide.shape[0] - count * steps
    for i in range(count):
        at = i * steps
        low, high = wide[at : at + steps], wide[skip + at : skip + at + steps]
        out[i] = jnp.where(core == 0, low, high).astype(BF16)


def local(tokens, gate_weight, up_weight, down_weight, decode_in):
    yz = lax.axis_index(("l", "a", "b", "c"))
    steps, rows, _ = decode_in.shape
    depth, ff = gate_weight.shape
    n_rows, block = tokens.shape
    n_dec = steps * rows
    width = down_weight.shape[1]
    each = -(-(n_rows + n_dec) // 32) * 16
    used, total = n_rows + n_dec, 2 * each

    decode_part = lax.dynamic_slice_in_dim(decode_in, yz * block, block, 2)
    feats = jnp.concatenate(
        [
            tokens.reshape(16, 2, 4, block).transpose(1, 0, 2, 3).reshape(n_rows, block),
            decode_part.transpose(1, 0, 2).reshape(n_dec, block),
            jnp.zeros((total - used, block), BF16),
        ],
        axis=0,
    )
    feats = lax.ppermute(
        feats, ("h", "b"), [(h * 4 + b, b * 4 + h) for h in range(4) for b in range(4)]
    )
    feats = exchange(jnp.broadcast_to(feats, (16, total, block)), LZ)
    own = call(weights_kernel, jax.ShapeDtypeStruct((2 * ff, depth), BF16), 1)(
        gate_weight.T, up_weight.T
    )
    own_near = near(own, "x")
    own_far = far(*own_near, "x", HINTS[0])
    opposite = lax.ppermute(down_weight, "h", [(i, (i + 2) % 4) for i in range(4)])
    feats, own_far = lax.optimization_barrier((feats, own_far))
    other = swap_cores(feats)

    weights = (own, own_near[0], *own_far, own_near[1])
    started = call(gate_up_start_kernel, jax.ShapeDtypeStruct((4 * total, 2 * ff), F32), HINTS[5])(feats, *weights)
    other, opposite = lax.optimization_barrier((other, opposite))
    partial, residue = call(
        gate_up_kernel,
        (
            jax.ShapeDtypeStruct((4, used, 2 * ff), BF16),
            jax.ShapeDtypeStruct((used, 2 * ff), BF16),
        ),
        HINTS[1],
    )(other, started, *weights)
    parts = exchange(partial, "h")
    hidden = call(hidden_kernel, jax.ShapeDtypeStruct((used, ff), BF16), 1)(parts, residue)
    beside = [(0, 1), (1, 0), (2, 3), (3, 2)]
    partner = lax.ppermute(hidden, "h", beside)
    down = call(pair_kernel, jax.ShapeDtypeStruct((2, ff, width), BF16), HINTS[3])(down_weight, opposite)
    down_near = near(down, "x")
    down_far = far(*down_near, "x", HINTS[2])
    weights = (down, down_near[0], *down_far, down_near[1])
    shape = (8, each, width)
    started = call(
        down_start_kernel,
        (jax.ShapeDtypeStruct(shape, F32), jax.ShapeDtypeStruct(shape, BF16)),
        HINTS[6],
    )(hidden, *weights)
    started, partner = lax.optimization_barrier((started, partner))
    shape = (8, 2, each, width)
    kept, given = call(
        down_kernel,
        (jax.ShapeDtypeStruct(shape, F32), jax.ShapeDtypeStruct(shape, BF16)),
        0.1,
    )(partner, *weights, *started)
    sums = (kept + swap_cores(given).astype(F32)).astype(BF16).reshape(16, each, width)

    half = n_rows // 2
    prefill = sums[:, :half].reshape(16, 16, 4, width).transpose(1, 0, 2, 3).reshape(16, half, width)
    sums = exchange(jnp.concatenate([prefill, sums[:, half:]], axis=1), LZ)
    sums = sums.astype(F32).sum(0).astype(BF16)
    decode_out = lax.ppermute(
        sums[half:],
        ("x", "h", "l", "a", "b"),
        [
            (
                x * 64 + h * 16 + q * 4 + k * 2 + r,
                q * 64 + (h ^ 2 * k) * 16 + x * 4 + (h ^ r),
            )
            for x in range(4)
            for h in range(4)
            for q in range(4)
            for k in range(2)
            for r in range(2)
        ],
    )
    decode_out = call(decode_kernel, jax.ShapeDtypeStruct((rows // 2, steps, width), BF16), HINTS[4])(decode_out)
    decode_out = decode_out.transpose(1, 0, 2)
    mine = sums[:half].reshape(4, 2, 2, 4, width)
    theirs = lax.ppermute(mine[:, :, 1], "h", beside)
    prefill_out = call(prefill_kernel, jax.ShapeDtypeStruct((4, 16 * width), BF16), 0.1)(mine[:, :, 0], theirs)
    return prefill_out, decode_out


def solution(mesh):
    sizes = [size for _, size in SIZES]
    fine = Mesh(mesh.devices.reshape(sizes), [name for name, _ in SIZES])
    gx, yz = GX, ("l", "a", "b", "c")
    return jax.shard_map(
        local,
        mesh=fine,
        in_specs=(P(gx, yz), P(gx, yz), P(gx, yz), P(yz, gx), P(None, gx, None)),
        out_specs=(P(gx + yz, None), P(None, yz, gx)),
        check_vma=False,
    )
```

```python
import jax
import jax.numpy as jnp
from jax import lax
from jax.experimental import pallas as pl
from jax.experimental.pallas import tpu as pltpu
from jax.sharding import Mesh, PartitionSpec as P

BF16 = jnp.bfloat16
F32 = jnp.float32
SIZES = (("x", 4), ("h", 4), ("l", 2), ("a", 2), ("b", 4), ("c", 2))
GX = ("x", "h")
LZ = ("l", "a", "b")
UP = [(i, (i + 1) % 4) for i in range(4)]
DOWN = [(i, (i + 3) % 4) for i in range(4)]
VMEM = 16 * 2**20
HINTS = (5.5, 0.1, 1, 0.1, 5, 8, 5, 5)


def swap_cores(value):
    return lax.ppermute(value, "c", [(0, 1), (1, 0)])


def exchange(blocks, axes):
    return lax.all_to_all(blocks, axes, split_axis=0, concat_axis=0, tiled=True)


def near(value, axis):
    return lax.ppermute(value, axis, DOWN), lax.ppermute(value, axis, UP)


def far(following, previous, axis, hint):
    shape = previous.shape[:-2] + (previous.shape[-2] // 2, previous.shape[-1])
    halves = jax.ShapeDtypeStruct(shape, BF16)
    up, down = call(halves_kernel, (halves, halves), hint)(previous, following)
    return lax.ppermute(up, axis, UP), lax.ppermute(down, axis, DOWN)


def call(kernel, outs, hint, scratch=(), vmem=VMEM, **more):
    return pl.pallas_call(
        kernel,
        out_shape=outs,
        scratch_shapes=list(scratch),
        compiler_params=pltpu.CompilerParams(vmem_limit_bytes=vmem),
        cost_estimate=pl.CostEstimate(flops=int(hint * 1.1e9), bytes_accessed=2**20, transcendentals=0),
        **more,
    )


def dot(lhs, rhs):
    return jnp.dot(lhs, rhs, preferred_element_type=F32)


def weights_kernel(gate, up, out):
    ff = gate.shape[0]
    even = ff // 128 * 128
    out[:even] = gate[:even]
    out[even : 2 * even] = up[:even]
    out[2 * even : even + ff] = gate[even:]
    out[even + ff :] = up[even:]


def rows_kernel(tokens, decode, out):
    count = tokens.shape[0]
    to = lax.broadcasted_iota(jnp.int32, (count, count), 0)
    source = lax.broadcasted_iota(jnp.int32, (count, count), 1)
    half = count // 2
    place = to % half // 4 * 8 + to // half * 4 + to % 4
    moved = dot((place == source).astype(BF16), tokens[...])
    fill = jnp.zeros((out.shape[0] - count - decode.shape[0], tokens.shape[1]), F32)
    out[...] = jnp.concatenate([moved, decode[...].astype(F32), fill], axis=0).astype(BF16)


def halves_kernel(previous, following, up, down):
    half = up.shape[-2]
    up[...] = previous[..., :half, :]
    down[...] = following[..., half:, :]


def pair_kernel(own, opposite, out):
    out[0] = own[...]
    out[1] = opposite[...]


def half_product(feats, weights, which):
    x = lax.axis_index("x")
    own, following, first, second, previous = weights
    block = feats.shape[2]
    part = pl.ds(pl.multiple_of(which * block, block), block)
    opposite = jnp.concatenate([first[:, part], second[:, part]], axis=0)
    rhs = jnp.concatenate([own[:, part], following[:, part], opposite, previous[:, part]], axis=1)
    lhs = [
        jnp.concatenate([feats[lax.rem(x + slot, 4) * 4 + b] for b in range(4)], axis=0) for slot in range(4)
    ]
    return lax.dot_general(
        jnp.concatenate(lhs, axis=1), rhs, (((1,), (1,)), ((), ())), preferred_element_type=F32
    )


def gate_up_start_kernel(feats, own, following, first, second, previous, out):
    out[...] = half_product(feats, (own, following, first, second, previous), lax.axis_index("c"))


def gate_up_kernel(feats, started, own, following, first, second, previous, partial, residue):
    h = lax.axis_index("h")
    blocks, rows, _ = partial.shape
    stride = feats.shape[1]
    weights = (own, following, first, second, previous)
    total = started[...] + half_product(feats, weights, 1 - lax.axis_index("c"))
    for b in range(blocks):
        part = total[b * stride : b * stride + rows]
        rounded = part.astype(BF16)
        partial[b] = rounded

        @pl.when(b == h)
        def _():
            residue[...] = (part - rounded.astype(F32)).astype(BF16)


def hidden_kernel(parts, residue, out):
    ff = out.shape[1]
    sums = residue[...].astype(F32)
    for source in range(4):
        sums = sums + parts[source].astype(F32)
    even = ff // 128 * 128
    gate, up, tail = sums[:, :even], sums[:, even : 2 * even], sums[:, 2 * even :]
    out[:, :even] = (gate / (1.0 + jnp.exp(-gate)) * up).astype(BF16)
    gate, up = tail[:, : ff - even], tail[:, ff - even :]
    out[:, even:] = (gate / (1.0 + jnp.exp(-gate)) * up).astype(BF16)


def down_products(half, hidden, own, following, first, second, previous, store):
    x, core = lax.axis_index("x"), lax.axis_index("c")
    mine = hidden[pl.ds(pl.multiple_of(core * half, 16), half)]
    other = hidden[pl.ds(pl.multiple_of((1 - core) * half, 16), half)]
    decode = hidden[2 * half :].astype(F32)
    low, high = decode[:16].astype(BF16), decode[8:].astype(BF16)
    lhs = jnp.concatenate(
        [mine, jnp.where(core == 0, low, high), other, jnp.where(core == 0, high, low)], axis=0
    )
    for slot in range(4):
        for k in range(2):
            if slot == 2:
                weight = jnp.concatenate([first[k], second[k]], axis=0)
            else:
                weight = (own, following, None, previous)[slot][k]
            terms = dot(lhs, weight)
            store(lax.rem(x + slot, 4) * 2 + k, terms[: half + 16], terms[half + 16 :].astype(BF16))


def down_start_kernel(hidden, own, following, first, second, previous, kept, given):
    def store(at, mine, other):
        kept[at] = mine
        given[at] = other

    down_products(kept.shape[1] - 16, hidden, own, following, first, second, previous, store)


def down_kernel(hidden, own, following, first, second, previous, kept0, given0, kept, given):
    def store(at, mine, other):
        kept[at, 1] = mine
        given[at, 1] = other

    down_products(kept.shape[2] - 16, hidden, own, following, first, second, previous, store)
    kept[:, 0] = kept0[...]
    given[:, 0] = given0[...]


def prefill_kernel(mine, theirs, out):
    h = lax.axis_index("h")
    width = mine.shape[3]
    for q in range(mine.shape[0]):
        for k in range(mine.shape[1]):
            column = lax.bitwise_xor(h, 2 * k)
            for ref, at in ((mine, column), (theirs, lax.bitwise_xor(column, 1))):
                out[:, pl.ds(pl.multiple_of((q * 4 + at) * width, width), width)] = ref[q, k]


def decode_kernel(rows, out):
    core = lax.axis_index("c")
    count, steps, _ = out.shape
    wide = rows[...].astype(F32)
    skip = wide.shape[0] - count * steps
    for i in range(count):
        at = i * steps
        low, high = wide[at : at + steps], wide[skip + at : skip + at + steps]
        out[i] = jnp.where(core == 0, low, high).astype(BF16)


def local(tokens, gate_weight, up_weight, down_weight, decode_in):
    yz = lax.axis_index(("l", "a", "b", "c"))
    steps, rows, _ = decode_in.shape
    depth, ff = gate_weight.shape
    n_rows, block = tokens.shape
    n_dec = steps * rows
    width = down_weight.shape[1]
    each = -(-(n_rows + n_dec) // 32) * 16
    used, total = n_rows + n_dec, 2 * each

    decode_part = lax.dynamic_slice_in_dim(decode_in, yz * block, block, 2)
    feats = call(rows_kernel, jax.ShapeDtypeStruct((total, block), BF16), HINTS[7])(
        tokens, decode_part.transpose(1, 0, 2).reshape(n_dec, block)
    )
    feats = lax.ppermute(
        feats, ("h", "b"), [(h * 4 + b, b * 4 + h) for h in range(4) for b in range(4)]
    )
    feats = exchange(jnp.broadcast_to(feats, (16, total, block)), LZ)
    own = call(weights_kernel, jax.ShapeDtypeStruct((2 * ff, depth), BF16), 1)(
        gate_weight.T, up_weight.T
    )
    own_near = near(own, "x")
    own_far = far(*own_near, "x", HINTS[0])
    opposite = lax.ppermute(down_weight, "h", [(i, (i + 2) % 4) for i in range(4)])
    feats, own_far = lax.optimization_barrier((feats, own_far))
    other = swap_cores(feats)

    weights = (own, own_near[0], *own_far, own_near[1])
    started = call(gate_up_start_kernel, jax.ShapeDtypeStruct((4 * total, 2 * ff), F32), HINTS[5])(feats, *weights)
    other, opposite = lax.optimization_barrier((other, opposite))
    partial, residue = call(
        gate_up_kernel,
        (
            jax.ShapeDtypeStruct((4, used, 2 * ff), BF16),
            jax.ShapeDtypeStruct((used, 2 * ff), BF16),
        ),
        HINTS[1],
    )(other, started, *weights)
    parts = exchange(partial, "h")
    hidden = call(hidden_kernel, jax.ShapeDtypeStruct((used, ff), BF16), 1)(parts, residue)
    beside = [(0, 1), (1, 0), (2, 3), (3, 2)]
    partner = lax.ppermute(hidden, "h", beside)
    down = call(pair_kernel, jax.ShapeDtypeStruct((2, ff, width), BF16), HINTS[3])(down_weight, opposite)
    down_near = near(down, "x")
    down_far = far(*down_near, "x", HINTS[2])
    weights = (down, down_near[0], *down_far, down_near[1])
    shape = (8, each, width)
    started = call(
        down_start_kernel,
        (jax.ShapeDtypeStruct(shape, F32), jax.ShapeDtypeStruct(shape, BF16)),
        HINTS[6],
    )(hidden, *weights)
    started, partner = lax.optimization_barrier((started, partner))
    shape = (8, 2, each, width)
    kept, given = call(
        down_kernel,
        (jax.ShapeDtypeStruct(shape, F32), jax.ShapeDtypeStruct(shape, BF16)),
        0.1,
    )(partner, *weights, *started)
    sums = (kept + swap_cores(given).astype(F32)).astype(BF16).reshape(16, each, width)

    half = n_rows // 2
    prefill = sums[:, :half].reshape(16, 16, 4, width).transpose(1, 0, 2, 3).reshape(16, half, width)
    sums = exchange(jnp.concatenate([prefill, sums[:, half:]], axis=1), LZ)
    sums = sums.astype(F32).sum(0).astype(BF16)
    decode_out = lax.ppermute(
        sums[half:],
        ("x", "h", "l", "a", "b"),
        [
            (
                x * 64 + h * 16 + q * 4 + k * 2 + r,
                q * 64 + (h ^ 2 * k) * 16 + x * 4 + (h ^ r),
            )
            for x in range(4)
            for h in range(4)
            for q in range(4)
            for k in range(2)
            for r in range(2)
        ],
    )
    decode_out = call(decode_kernel, jax.ShapeDtypeStruct((rows // 2, steps, width), BF16), HINTS[4])(decode_out)
    decode_out = decode_out.transpose(1, 0, 2)
    mine = sums[:half].reshape(4, 2, 2, 4, width)
    theirs = lax.ppermute(mine[:, :, 1], "h", beside)
    prefill_out = call(prefill_kernel, jax.ShapeDtypeStruct((4, 16 * width), BF16), 0.1)(mine[:, :, 0], theirs)
    return prefill_out, decode_out


def solution(mesh):
    sizes = [size for _, size in SIZES]
    fine = Mesh(mesh.devices.reshape(sizes), [name for name, _ in SIZES])
    gx, yz = GX, ("l", "a", "b", "c")
    return jax.shard_map(
        local,
        mesh=fine,
        in_specs=(P(gx, yz), P(gx, yz), P(gx, yz), P(yz, gx), P(None, gx, None)),
        out_specs=(P(gx + yz, None), P(None, yz, gx)),
        check_vma=False,
    )
```

```python
import jax
import jax.numpy as jnp
from jax import lax
from jax.experimental import pallas as pl
from jax.experimental.pallas import tpu as pltpu
from jax.sharding import Mesh, PartitionSpec as P

BF16 = jnp.bfloat16
F32 = jnp.float32
SIZES = (("x", 4), ("h", 4), ("l", 2), ("a", 2), ("b", 4), ("c", 2))
GX = ("x", "h")
LZ = ("l", "a", "b")
UP = [(i, (i + 1) % 4) for i in range(4)]
DOWN = [(i, (i + 3) % 4) for i in range(4)]
VMEM = 16 * 2**20
HINTS = (4.95, 0.1, 1, 0.1, 5, 8, 5, 5)


def swap_cores(value):
    return lax.ppermute(value, "c", [(0, 1), (1, 0)])


def exchange(blocks, axes):
    return lax.all_to_all(blocks, axes, split_axis=0, concat_axis=0, tiled=True)


def near(value, axis):
    return lax.ppermute(value, axis, DOWN), lax.ppermute(value, axis, UP)


def far(following, previous, axis, hint):
    shape = previous.shape[:-2] + (previous.shape[-2] // 2, previous.shape[-1])
    halves = jax.ShapeDtypeStruct(shape, BF16)
    up, down = call(halves_kernel, (halves, halves), hint)(previous, following)
    return lax.ppermute(up, axis, UP), lax.ppermute(down, axis, DOWN)


def call(kernel, outs, hint, scratch=(), vmem=VMEM, **more):
    return pl.pallas_call(
        kernel,
        out_shape=outs,
        scratch_shapes=list(scratch),
        compiler_params=pltpu.CompilerParams(vmem_limit_bytes=vmem),
        cost_estimate=pl.CostEstimate(flops=int(hint * 1.1e9), bytes_accessed=2**20, transcendentals=0),
        **more,
    )


def dot(lhs, rhs):
    return jnp.dot(lhs, rhs, preferred_element_type=F32)


def weights_kernel(gate, up, out):
    ff = gate.shape[0]
    even = ff // 128 * 128
    out[:even] = gate[:even]
    out[even : 2 * even] = up[:even]
    out[2 * even : even + ff] = gate[even:]
    out[even + ff :] = up[even:]


def rows_kernel(tokens, decode, out):
    count = tokens.shape[0]
    to = lax.broadcasted_iota(jnp.int32, (count, count), 0)
    source = lax.broadcasted_iota(jnp.int32, (count, count), 1)
    half = count // 2
    place = to % half // 4 * 8 + to // half * 4 + to % 4
    moved = dot((place == source).astype(BF16), tokens[...])
    out[...] = jnp.concatenate([moved, decode[...].astype(F32)], axis=0).astype(BF16)


def halves_kernel(previous, following, up, down):
    half = up.shape[-2]
    up[...] = previous[..., :half, :]
    down[...] = following[..., half:, :]


def pair_kernel(own, opposite, out):
    out[0] = own[...]
    out[1] = opposite[...]


def half_product(feats, weights, which):
    x = lax.axis_index("x")
    own, following, first, second, previous = weights
    block = feats.shape[2]
    part = pl.ds(pl.multiple_of(which * block, block), block)
    opposite = jnp.concatenate([first[:, part], second[:, part]], axis=0)
    rhs = jnp.concatenate([own[:, part], following[:, part], opposite, previous[:, part]], axis=1)
    fill = jnp.zeros((-feats.shape[1] % 16, block), BF16)
    lhs = [
        jnp.concatenate(
            [part for b in range(4) for part in (feats[lax.rem(x + slot, 4) * 4 + b], fill)], axis=0
        )
        for slot in range(4)
    ]
    return lax.dot_general(
        jnp.concatenate(lhs, axis=1), rhs, (((1,), (1,)), ((), ())), preferred_element_type=F32
    )


def gate_up_start_kernel(feats, own, following, first, second, previous, out):
    out[...] = half_product(feats, (own, following, first, second, previous), lax.axis_index("c"))


def gate_up_kernel(feats, started, own, following, first, second, previous, partial, residue):
    h = lax.axis_index("h")
    blocks, rows, _ = partial.shape
    weights = (own, following, first, second, previous)
    total = started[...] + half_product(feats, weights, 1 - lax.axis_index("c"))
    stride = total.shape[0] // blocks
    for b in range(blocks):
        part = total[b * stride : b * stride + rows]
        rounded = part.astype(BF16)
        partial[b] = rounded

        @pl.when(b == h)
        def _():
            residue[...] = (part - rounded.astype(F32)).astype(BF16)


def hidden_kernel(parts, residue, out):
    ff = out.shape[1]
    sums = residue[...].astype(F32)
    for source in range(4):
        sums = sums + parts[source].astype(F32)
    even = ff // 128 * 128
    gate, up, tail = sums[:, :even], sums[:, even : 2 * even], sums[:, 2 * even :]
    out[:, :even] = (gate / (1.0 + jnp.exp(-gate)) * up).astype(BF16)
    gate, up = tail[:, : ff - even], tail[:, ff - even :]
    out[:, even:] = (gate / (1.0 + jnp.exp(-gate)) * up).astype(BF16)


def down_products(half, hidden, own, following, first, second, previous, store):
    x, core = lax.axis_index("x"), lax.axis_index("c")
    mine = hidden[pl.ds(pl.multiple_of(core * half, 16), half)]
    other = hidden[pl.ds(pl.multiple_of((1 - core) * half, 16), half)]
    decode = hidden[2 * half :].astype(F32)
    low, high = decode[:16].astype(BF16), decode[8:].astype(BF16)
    lhs = jnp.concatenate(
        [mine, jnp.where(core == 0, low, high), other, jnp.where(core == 0, high, low)], axis=0
    )
    for slot in range(4):
        for k in range(2):
            if slot == 2:
                weight = jnp.concatenate([first[k], second[k]], axis=0)
            else:
                weight = (own, following, None, previous)[slot][k]
            terms = dot(lhs, weight)
            store(lax.rem(x + slot, 4) * 2 + k, terms[: half + 16], terms[half + 16 :].astype(BF16))


def down_start_kernel(hidden, own, following, first, second, previous, kept, given):
    def store(at, mine, other):
        kept[at] = mine
        given[at] = other

    down_products(kept.shape[1] - 16, hidden, own, following, first, second, previous, store)


def down_kernel(hidden, own, following, first, second, previous, kept0, given0, kept, given):
    def store(at, mine, other):
        kept[at, 1] = mine
        given[at, 1] = other

    down_products(kept.shape[2] - 16, hidden, own, following, first, second, previous, store)
    kept[:, 0] = kept0[...]
    given[:, 0] = given0[...]


def prefill_kernel(mine, theirs, out):
    h = lax.axis_index("h")
    width = mine.shape[3]
    for q in range(mine.shape[0]):
        for k in range(mine.shape[1]):
            column = lax.bitwise_xor(h, 3 * k)
            for ref, at in ((mine, column), (theirs, lax.bitwise_xor(column, 1))):
                out[:, pl.ds(pl.multiple_of((q * 4 + at) * width, width), width)] = ref[q, k]


def decode_kernel(rows, out):
    core = lax.axis_index("c")
    count, steps, _ = out.shape
    wide = rows[...].astype(F32)
    skip = wide.shape[0] - count * steps
    for i in range(count):
        at = i * steps
        low, high = wide[at : at + steps], wide[skip + at : skip + at + steps]
        out[i] = jnp.where(core == 0, low, high).astype(BF16)


def local(tokens, gate_weight, up_weight, down_weight, decode_in):
    yz = lax.axis_index(("l", "a", "b", "c"))
    steps, rows, _ = decode_in.shape
    depth, ff = gate_weight.shape
    n_rows, block = tokens.shape
    n_dec = steps * rows
    width = down_weight.shape[1]
    each = -(-(n_rows + n_dec) // 32) * 16
    used, total = n_rows + n_dec, 2 * each

    decode_part = lax.dynamic_slice_in_dim(decode_in, yz * block, block, 2)
    feats = call(rows_kernel, jax.ShapeDtypeStruct((used, block), BF16), HINTS[7])(
        tokens, decode_part.transpose(1, 0, 2).reshape(n_dec, block)
    )
    feats = lax.ppermute(
        feats, ("h", "b"), [(h * 4 + b, b * 4 + h) for h in range(4) for b in range(4)]
    )
    feats = exchange(jnp.broadcast_to(feats, (16, used, block)), LZ)
    own = call(weights_kernel, jax.ShapeDtypeStruct((2 * ff, depth), BF16), 1)(
        gate_weight.T, up_weight.T
    )
    own_near = near(own, "x")
    own_far = far(*own_near, "x", HINTS[0])
    opposite = lax.ppermute(down_weight, "h", [(i, 3 - i) for i in range(4)])
    feats, own_far = lax.optimization_barrier((feats, own_far))
    other = swap_cores(feats)

    weights = (own, own_near[0], *own_far, own_near[1])
    started = call(gate_up_start_kernel, jax.ShapeDtypeStruct((4 * total, 2 * ff), F32), HINTS[5])(feats, *weights)
    other, opposite = lax.optimization_barrier((other, opposite))
    partial, residue = call(
        gate_up_kernel,
        (
            jax.ShapeDtypeStruct((4, used, 2 * ff), BF16),
            jax.ShapeDtypeStruct((used, 2 * ff), BF16),
        ),
        HINTS[1],
    )(other, started, *weights)
    parts = exchange(partial, "h")
    hidden = call(hidden_kernel, jax.ShapeDtypeStruct((used, ff), BF16), 1)(parts, residue)
    beside = [(0, 1), (1, 0), (2, 3), (3, 2)]
    partner = lax.ppermute(hidden, "h", beside)
    down = call(pair_kernel, jax.ShapeDtypeStruct((2, ff, width), BF16), HINTS[3])(down_weight, opposite)
    down_near = near(down, "x")
    down_far = far(*down_near, "x", HINTS[2])
    weights = (down, down_near[0], *down_far, down_near[1])
    shape = (8, each, width)
    started = call(
        down_start_kernel,
        (jax.ShapeDtypeStruct(shape, F32), jax.ShapeDtypeStruct(shape, BF16)),
        HINTS[6],
    )(hidden, *weights)
    started, partner = lax.optimization_barrier((started, partner))
    shape = (8, 2, each, width)
    kept, given = call(
        down_kernel,
        (jax.ShapeDtypeStruct(shape, F32), jax.ShapeDtypeStruct(shape, BF16)),
        0.1,
    )(partner, *weights, *started)
    sums = (kept + swap_cores(given).astype(F32)).astype(BF16).reshape(16, each, width)

    half = n_rows // 2
    prefill = sums[:, :half].reshape(16, 16, 4, width).transpose(1, 0, 2, 3).reshape(16, half, width)
    sums = exchange(jnp.concatenate([prefill, sums[:, half:]], axis=1), LZ)
    sums = sums.astype(F32).sum(0).astype(BF16)
    decode_out = lax.ppermute(
        sums[half:],
        ("x", "h", "l", "a", "b"),
        [
            (
                x * 64 + h * 16 + q * 4 + k * 2 + r,
                q * 64 + (h ^ 3 * k) * 16 + x * 4 + (h ^ r),
            )
            for x in range(4)
            for h in range(4)
            for q in range(4)
            for k in range(2)
            for r in range(2)
        ],
    )
    decode_out = call(decode_kernel, jax.ShapeDtypeStruct((rows // 2, steps, width), BF16), HINTS[4])(decode_out)
    decode_out = decode_out.transpose(1, 0, 2)
    mine = sums[:half].reshape(4, 2, 2, 4, width)
    theirs = lax.ppermute(mine[:, :, 1], "h", beside)
    prefill_out = call(prefill_kernel, jax.ShapeDtypeStruct((4, 16 * width), BF16), 0.1)(mine[:, :, 0], theirs)
    return prefill_out, decode_out


def solution(mesh):
    sizes = [size for _, size in SIZES]
    fine = Mesh(mesh.devices.reshape(sizes), [name for name, _ in SIZES])
    gx, yz = GX, ("l", "a", "b", "c")
    return jax.shard_map(
        local,
        mesh=fine,
        in_specs=(P(gx, yz), P(gx, yz), P(gx, yz), P(yz, gx), P(None, gx, None)),
        out_specs=(P(gx + yz, None), P(None, yz, gx)),
        check_vma=False,
    )
```

```python
import jax
import jax.numpy as jnp
from jax import lax
from jax.experimental import pallas as pl
from jax.experimental.pallas import tpu as pltpu
from jax.sharding import Mesh, PartitionSpec as P

BF16 = jnp.bfloat16
F32 = jnp.float32
SIZES = (("x", 4), ("h", 4), ("l", 2), ("a", 2), ("b", 4), ("c", 2))
GX = ("x", "h")
LZ = ("l", "a", "b")
UP = [(i, (i + 1) % 4) for i in range(4)]
DOWN = [(i, (i + 3) % 4) for i in range(4)]
VMEM = 10 * 2**20
HINTS = (4.95, 0.1, 1, 0.1, 5, 8, 5, 5)


def swap_cores(value):
    return lax.ppermute(value, "c", [(0, 1), (1, 0)])


def exchange(blocks, axes):
    return lax.all_to_all(blocks, axes, split_axis=0, concat_axis=0, tiled=True)


def near(value, axis):
    return lax.ppermute(value, axis, DOWN), lax.ppermute(value, axis, UP)


def far(following, previous, axis, hint):
    shape = previous.shape[:-2] + (previous.shape[-2] // 2, previous.shape[-1])
    halves = jax.ShapeDtypeStruct(shape, BF16)
    up, down = call(halves_kernel, (halves, halves), hint)(previous, following)
    return lax.ppermute(up, axis, UP), lax.ppermute(down, axis, DOWN)


def call(kernel, outs, hint, scratch=(), vmem=VMEM, **more):
    return pl.pallas_call(
        kernel,
        out_shape=outs,
        scratch_shapes=list(scratch),
        compiler_params=pltpu.CompilerParams(vmem_limit_bytes=vmem),
        cost_estimate=pl.CostEstimate(flops=int(hint * 1.1e9), bytes_accessed=2**20, transcendentals=0),
        **more,
    )


def dot(lhs, rhs):
    return jnp.dot(lhs, rhs, preferred_element_type=F32)


def weights_kernel(gate, up, out):
    ff = gate.shape[0]
    even = ff // 128 * 128
    out[:even] = gate[:even]
    out[even : 2 * even] = up[:even]
    out[2 * even : even + ff] = gate[even:]
    out[even + ff :] = up[even:]


def rows_kernel(tokens, decode, out):
    count = tokens.shape[0]
    to = lax.broadcasted_iota(jnp.int32, (count, count), 0)
    source = lax.broadcasted_iota(jnp.int32, (count, count), 1)
    half = count // 2
    place = to % half // 4 * 8 + to // half * 4 + to % 4
    moved = dot((place == source).astype(BF16), tokens[...])
    out[...] = jnp.concatenate([moved, decode[...].astype(F32)], axis=0).astype(BF16)


def halves_kernel(previous, following, up, down):
    half = up.shape[-2]
    up[...] = previous[..., :half, :]
    down[...] = following[..., half:, :]


def pair_kernel(own, opposite, out):
    out[0] = own[...]
    out[1] = opposite[...]


def half_product(feats, weights, which):
    x = lax.axis_index("x")
    own, following, first, second, previous = weights
    block = feats.shape[2]
    part = pl.ds(pl.multiple_of(which * block, block), block)
    opposite = jnp.concatenate([first[:, part], second[:, part]], axis=0)
    rhs = jnp.concatenate([own[:, part], following[:, part], opposite, previous[:, part]], axis=1)
    fill = jnp.zeros((-feats.shape[1] % 16, block), BF16)
    lhs = [
        jnp.concatenate(
            [part for b in range(4) for part in (feats[lax.rem(x + slot, 4) * 4 + b], fill)], axis=0
        )
        for slot in range(4)
    ]
    return lax.dot_general(
        jnp.concatenate(lhs, axis=1), rhs, (((1,), (1,)), ((), ())), preferred_element_type=F32
    )


def gate_up_start_kernel(feats, own, following, first, second, previous, out):
    out[...] = half_product(feats, (own, following, first, second, previous), lax.axis_index("c"))


def gate_up_kernel(feats, started, own, following, first, second, previous, partial, residue):
    h = lax.axis_index("h")
    blocks, rows, _ = partial.shape
    weights = (own, following, first, second, previous)
    total = started[...] + half_product(feats, weights, 1 - lax.axis_index("c"))
    stride = total.shape[0] // blocks
    for b in range(blocks):
        part = total[b * stride : b * stride + rows]
        rounded = part.astype(BF16)
        partial[b] = rounded

        @pl.when(b == h)
        def _():
            residue[...] = (part - rounded.astype(F32)).astype(BF16)


def hidden_kernel(parts, residue, out):
    ff = out.shape[1]
    sums = residue[...].astype(F32)
    for source in range(4):
        sums = sums + parts[source].astype(F32)
    even = ff // 128 * 128
    gate, up, tail = sums[:, :even], sums[:, even : 2 * even], sums[:, 2 * even :]
    out[:, :even] = (gate / (1.0 + jnp.exp(-gate)) * up).astype(BF16)
    gate, up = tail[:, : ff - even], tail[:, ff - even :]
    out[:, even:] = (gate / (1.0 + jnp.exp(-gate)) * up).astype(BF16)


def down_products(half, hidden, own, following, first, second, previous, store):
    x, core = lax.axis_index("x"), lax.axis_index("c")
    mine = hidden[pl.ds(pl.multiple_of(core * half, 16), half)]
    other = hidden[pl.ds(pl.multiple_of((1 - core) * half, 16), half)]
    decode = hidden[2 * half :].astype(F32)
    low, high = decode[:16].astype(BF16), decode[8:].astype(BF16)
    lhs = jnp.concatenate(
        [mine, jnp.where(core == 0, low, high), other, jnp.where(core == 0, high, low)], axis=0
    )
    for slot in range(4):
        for k in range(2):
            if slot == 2:
                weight = jnp.concatenate([first[k], second[k]], axis=0)
            else:
                weight = (own, following, None, previous)[slot][k]
            terms = dot(lhs, weight)
            store(lax.rem(x + slot, 4) * 2 + k, terms[: half + 16], terms[half + 16 :].astype(BF16))


def down_start_kernel(hidden, own, following, first, second, previous, kept, given):
    def store(at, mine, other):
        kept[at] = mine
        given[at] = other

    down_products(kept.shape[1] - 16, hidden, own, following, first, second, previous, store)


def down_kernel(hidden, own, following, first, second, previous, kept0, given0, kept, given):
    def store(at, mine, other):
        kept[at, 1] = mine
        given[at, 1] = other

    down_products(kept.shape[2] - 16, hidden, own, following, first, second, previous, store)
    kept[:, 0] = kept0[...]
    given[:, 0] = given0[...]


def prefill_kernel(mine, theirs, out):
    h = lax.axis_index("h")
    width = mine.shape[3]
    for q in range(mine.shape[0]):
        for k in range(mine.shape[1]):
            column = lax.bitwise_xor(h, 3 * k)
            for ref, at in ((mine, column), (theirs, lax.bitwise_xor(column, 1))):
                out[:, pl.ds(pl.multiple_of((q * 4 + at) * width, width), width)] = ref[q, k]


def decode_kernel(rows, out):
    core = lax.axis_index("c")
    count, steps, _ = out.shape
    wide = rows[...].astype(F32)
    skip = wide.shape[0] - count * steps
    for i in range(count):
        at = i * steps
        low, high = wide[at : at + steps], wide[skip + at : skip + at + steps]
        out[i] = jnp.where(core == 0, low, high).astype(BF16)


def local(tokens, gate_weight, up_weight, down_weight, decode_in):
    yz = lax.axis_index(("l", "a", "b", "c"))
    steps, rows, _ = decode_in.shape
    depth, ff = gate_weight.shape
    n_rows, block = tokens.shape
    n_dec = steps * rows
    width = down_weight.shape[1]
    each = -(-(n_rows + n_dec) // 32) * 16
    used, total = n_rows + n_dec, 2 * each

    decode_part = lax.dynamic_slice_in_dim(decode_in, yz * block, block, 2)
    feats = call(rows_kernel, jax.ShapeDtypeStruct((used, block), BF16), HINTS[7])(
        tokens, decode_part.transpose(1, 0, 2).reshape(n_dec, block)
    )
    feats = lax.ppermute(
        feats, ("h", "b"), [(h * 4 + b, b * 4 + h) for h in range(4) for b in range(4)]
    )
    feats = exchange(jnp.broadcast_to(feats, (16, used, block)), LZ)
    own = call(weights_kernel, jax.ShapeDtypeStruct((2 * ff, depth), BF16), 1)(
        gate_weight.T, up_weight.T
    )
    own_near = near(own, "x")
    own_far = far(*own_near, "x", HINTS[0])
    opposite = lax.ppermute(down_weight, "h", [(i, 3 - i) for i in range(4)])
    feats, own_far = lax.optimization_barrier((feats, own_far))
    other = swap_cores(feats)

    weights = (own, own_near[0], *own_far, own_near[1])
    started = call(gate_up_start_kernel, jax.ShapeDtypeStruct((4 * total, 2 * ff), F32), HINTS[5])(feats, *weights)
    other, opposite = lax.optimization_barrier((other, opposite))
    partial, residue = call(
        gate_up_kernel,
        (
            jax.ShapeDtypeStruct((4, used, 2 * ff), BF16),
            jax.ShapeDtypeStruct((used, 2 * ff), BF16),
        ),
        HINTS[1],
    )(other, started, *weights)
    parts = exchange(partial, "h")
    hidden = call(hidden_kernel, jax.ShapeDtypeStruct((used, ff), BF16), 1)(parts, residue)
    beside = [(0, 1), (1, 0), (2, 3), (3, 2)]
    partner = lax.ppermute(hidden, "h", beside)
    down = call(pair_kernel, jax.ShapeDtypeStruct((2, ff, width), BF16), HINTS[3])(down_weight, opposite)
    down_near = near(down, "x")
    down_far = far(*down_near, "x", HINTS[2])
    weights = (down, down_near[0], *down_far, down_near[1])
    shape = (8, each, width)
    started = call(
        down_start_kernel,
        (jax.ShapeDtypeStruct(shape, F32), jax.ShapeDtypeStruct(shape, BF16)),
        HINTS[6],
    )(hidden, *weights)
    started, partner = lax.optimization_barrier((started, partner))
    shape = (8, 2, each, width)
    kept, given = call(
        down_kernel,
        (jax.ShapeDtypeStruct(shape, F32), jax.ShapeDtypeStruct(shape, BF16)),
        0.1,
    )(partner, *weights, *started)
    sums = (kept + swap_cores(given).astype(F32)).astype(BF16).reshape(16, each, width)

    half = n_rows // 2
    prefill = sums[:, :half].reshape(16, 16, 4, width).transpose(1, 0, 2, 3).reshape(16, half, width)
    sums = exchange(jnp.concatenate([prefill, sums[:, half:]], axis=1), LZ)
    sums = sums.astype(F32).sum(0).astype(BF16)
    decode_out = lax.ppermute(
        sums[half:],
        ("x", "h", "l", "a", "b"),
        [
            (
                x * 64 + h * 16 + q * 4 + k * 2 + r,
                q * 64 + (h ^ 3 * k) * 16 + x * 4 + (h ^ r),
            )
            for x in range(4)
            for h in range(4)
            for q in range(4)
            for k in range(2)
            for r in range(2)
        ],
    )
    decode_out = call(decode_kernel, jax.ShapeDtypeStruct((rows // 2, steps, width), BF16), HINTS[4])(decode_out)
    decode_out = decode_out.transpose(1, 0, 2)
    mine = sums[:half].reshape(4, 2, 2, 4, width)
    theirs = lax.ppermute(mine[:, :, 1], "h", beside)
    prefill_out = call(prefill_kernel, jax.ShapeDtypeStruct((4, 16 * width), BF16), 0.1)(mine[:, :, 0], theirs)
    return prefill_out, decode_out


def solution(mesh):
    sizes = [size for _, size in SIZES]
    fine = Mesh(mesh.devices.reshape(sizes), [name for name, _ in SIZES])
    gx, yz = GX, ("l", "a", "b", "c")
    return jax.shard_map(
        local,
        mesh=fine,
        in_specs=(P(gx, yz), P(gx, yz), P(gx, yz), P(yz, gx), P(None, gx, None)),
        out_specs=(P(gx + yz, None), P(None, yz, gx)),
        check_vma=False,
    )
```

```python
import jax
import jax.numpy as jnp
from jax import lax
from jax.experimental import pallas as pl
from jax.experimental.pallas import tpu as pltpu
from jax.sharding import Mesh, PartitionSpec as P

BF16 = jnp.bfloat16
F32 = jnp.float32
SIZES = (("x", 4), ("h", 4), ("l", 2), ("a", 2), ("b", 4), ("c", 2))
GX = ("x", "h")
LZ = ("l", "a", "b")
UP = [(i, (i + 1) % 4) for i in range(4)]
DOWN = [(i, (i + 3) % 4) for i in range(4)]
VMEM = 10 * 2**20
HINTS = (4.95, 0.1, 1, 10, 5, 8, 5, 5)


def swap_cores(value):
    return lax.ppermute(value, "c", [(0, 1), (1, 0)])


def exchange(blocks, axes):
    return lax.all_to_all(blocks, axes, split_axis=0, concat_axis=0, tiled=True)


def near(value, axis):
    return lax.ppermute(value, axis, DOWN), lax.ppermute(value, axis, UP)


def far(following, previous, axis, hint):
    shape = previous.shape[:-2] + (previous.shape[-2] // 2, previous.shape[-1])
    halves = jax.ShapeDtypeStruct(shape, BF16)
    up, down = call(halves_kernel, (halves, halves), hint)(previous, following)
    return lax.ppermute(up, axis, UP), lax.ppermute(down, axis, DOWN)


def call(kernel, outs, hint, scratch=(), vmem=VMEM, **more):
    return pl.pallas_call(
        kernel,
        out_shape=outs,
        scratch_shapes=list(scratch),
        compiler_params=pltpu.CompilerParams(vmem_limit_bytes=vmem),
        cost_estimate=pl.CostEstimate(flops=int(hint * 1.1e9), bytes_accessed=2**20, transcendentals=0),
        **more,
    )


def dot(lhs, rhs):
    return jnp.dot(lhs, rhs, preferred_element_type=F32)


def weights_kernel(gate, up, out):
    ff = gate.shape[0]
    even = ff // 128 * 128
    out[:even] = gate[:even]
    out[even : 2 * even] = up[:even]
    out[2 * even : even + ff] = gate[even:]
    out[even + ff :] = up[even:]


def rows_kernel(tokens, decode, out):
    count = tokens.shape[0]
    to = lax.broadcasted_iota(jnp.int32, (count, count), 0)
    source = lax.broadcasted_iota(jnp.int32, (count, count), 1)
    half = count // 2
    place = to % half // 4 * 8 + to // half * 4 + to % 4
    moved = dot((place == source).astype(BF16), tokens[...])
    out[...] = jnp.concatenate([moved, decode[...].astype(F32)], axis=0).astype(BF16)


def halves_kernel(previous, following, up, down):
    half = up.shape[-2]
    up[...] = previous[..., :half, :]
    down[...] = following[..., half:, :]


def pair_kernel(own, opposite, out):
    out[0] = own[...]
    out[1] = opposite[...]


def half_product(feats, weights, which):
    x = lax.axis_index("x")
    own, following, first, second, previous = weights
    block = feats.shape[2]
    part = pl.ds(pl.multiple_of(which * block, block), block)
    opposite = jnp.concatenate([first[:, part], second[:, part]], axis=0)
    rhs = jnp.concatenate([own[:, part], following[:, part], opposite, previous[:, part]], axis=1)
    fill = jnp.zeros((-feats.shape[1] % 16, block), BF16)
    lhs = [
        jnp.concatenate(
            [part for b in range(4) for part in (feats[lax.rem(x + slot, 4) * 4 + b], fill)], axis=0
        )
        for slot in range(4)
    ]
    return lax.dot_general(
        jnp.concatenate(lhs, axis=1), rhs, (((1,), (1,)), ((), ())), preferred_element_type=F32
    )


def gate_up_start_kernel(feats, own, following, first, second, previous, out):
    out[...] = half_product(feats, (own, following, first, second, previous), lax.axis_index("c"))


def gate_up_kernel(feats, started, own, following, first, second, previous, partial, residue):
    h = lax.axis_index("h")
    blocks, rows, _ = partial.shape
    weights = (own, following, first, second, previous)
    total = started[...] + half_product(feats, weights, 1 - lax.axis_index("c"))
    stride = total.shape[0] // blocks
    for b in range(blocks):
        part = total[b * stride : b * stride + rows]
        rounded = part.astype(BF16)
        partial[b] = rounded

        @pl.when(b == h)
        def _():
            residue[...] = (part - rounded.astype(F32)).astype(BF16)


def hidden_kernel(parts, residue, out):
    ff = out.shape[1]
    sums = residue[...].astype(F32)
    for source in range(4):
        sums = sums + parts[source].astype(F32)
    even = ff // 128 * 128
    gate, up, tail = sums[:, :even], sums[:, even : 2 * even], sums[:, 2 * even :]
    out[:, :even] = (gate / (1.0 + jnp.exp(-gate)) * up).astype(BF16)
    gate, up = tail[:, : ff - even], tail[:, ff - even :]
    out[:, even:] = (gate / (1.0 + jnp.exp(-gate)) * up).astype(BF16)


def down_products(half, hidden, own, following, first, second, previous, store):
    x, core = lax.axis_index("x"), lax.axis_index("c")
    mine = hidden[pl.ds(pl.multiple_of(core * half, 16), half)]
    other = hidden[pl.ds(pl.multiple_of((1 - core) * half, 16), half)]
    decode = hidden[2 * half :].astype(F32)
    low, high = decode[:16].astype(BF16), decode[8:].astype(BF16)
    lhs = jnp.concatenate(
        [mine, jnp.where(core == 0, low, high), other, jnp.where(core == 0, high, low)], axis=0
    )
    for slot in range(4):
        for k in range(2):
            if slot == 2:
                weight = jnp.concatenate([first[k], second[k]], axis=0)
            else:
                weight = (own, following, None, previous)[slot][k]
            terms = dot(lhs, weight)
            store(lax.rem(x + slot, 4) * 2 + k, terms[: half + 16], terms[half + 16 :].astype(BF16))


def down_start_kernel(hidden, own, following, first, second, previous, kept, given):
    def store(at, mine, other):
        kept[at] = mine
        given[at] = other

    down_products(kept.shape[1] - 16, hidden, own, following, first, second, previous, store)


def down_kernel(hidden, own, following, first, second, previous, kept0, given0, kept, given):
    def store(at, mine, other):
        kept[at, 1] = mine
        given[at, 1] = other

    down_products(kept.shape[2] - 16, hidden, own, following, first, second, previous, store)
    kept[:, 0] = kept0[...]
    given[:, 0] = given0[...]


def prefill_kernel(mine, theirs, out):
    h = lax.axis_index("h")
    width = mine.shape[3]
    for q in range(mine.shape[0]):
        for k in range(mine.shape[1]):
            column = lax.bitwise_xor(h, 3 * k)
            for ref, at in ((mine, column), (theirs, lax.bitwise_xor(column, 1))):
                out[:, pl.ds(pl.multiple_of((q * 4 + at) * width, width), width)] = ref[q, k]


def decode_kernel(rows, out):
    core = lax.axis_index("c")
    count, steps, _ = out.shape
    wide = rows[...].astype(F32)
    skip = wide.shape[0] - count * steps
    for i in range(count):
        at = i * steps
        low, high = wide[at : at + steps], wide[skip + at : skip + at + steps]
        out[i] = jnp.where(core == 0, low, high).astype(BF16)


def local(tokens, gate_weight, up_weight, down_weight, decode_in):
    yz = lax.axis_index(("l", "a", "b", "c"))
    steps, rows, _ = decode_in.shape
    depth, ff = gate_weight.shape
    n_rows, block = tokens.shape
    n_dec = steps * rows
    width = down_weight.shape[1]
    each = -(-(n_rows + n_dec) // 32) * 16
    used, total = n_rows + n_dec, 2 * each

    decode_part = lax.dynamic_slice_in_dim(decode_in, yz * block, block, 2)
    feats = call(rows_kernel, jax.ShapeDtypeStruct((used, block), BF16), HINTS[7])(
        tokens, decode_part.transpose(1, 0, 2).reshape(n_dec, block)
    )
    feats = lax.ppermute(
        feats, ("h", "b"), [(h * 4 + b, b * 4 + h) for h in range(4) for b in range(4)]
    )
    feats = exchange(jnp.broadcast_to(feats, (16, used, block)), LZ)
    own = call(weights_kernel, jax.ShapeDtypeStruct((2 * ff, depth), BF16), 1)(
        gate_weight.T, up_weight.T
    )
    own_near = near(own, "x")
    own_far = far(*own_near, "x", HINTS[0])
    opposite = lax.ppermute(down_weight, "h", [(i, 3 - i) for i in range(4)])
    feats, own_far = lax.optimization_barrier((feats, own_far))
    other = swap_cores(feats)

    weights = (own, own_near[0], *own_far, own_near[1])
    started = call(gate_up_start_kernel, jax.ShapeDtypeStruct((4 * total, 2 * ff), F32), HINTS[5])(feats, *weights)
    partial, residue = call(
        gate_up_kernel,
        (
            jax.ShapeDtypeStruct((4, used, 2 * ff), BF16),
            jax.ShapeDtypeStruct((used, 2 * ff), BF16),
        ),
        HINTS[1],
    )(other, started, *weights)
    parts = exchange(partial, "h")
    hidden = call(hidden_kernel, jax.ShapeDtypeStruct((used, ff), BF16), 1)(parts, residue)
    beside = [(0, 1), (1, 0), (2, 3), (3, 2)]
    partner = lax.ppermute(hidden, "h", beside)
    down = call(pair_kernel, jax.ShapeDtypeStruct((2, ff, width), BF16), HINTS[3])(down_weight, opposite)
    down_near = near(down, "x")
    down_far = far(*down_near, "x", HINTS[2])
    weights = (down, down_near[0], *down_far, down_near[1])
    shape = (8, each, width)
    started = call(
        down_start_kernel,
        (jax.ShapeDtypeStruct(shape, F32), jax.ShapeDtypeStruct(shape, BF16)),
        HINTS[6],
    )(hidden, *weights)
    started, partner = lax.optimization_barrier((started, partner))
    shape = (8, 2, each, width)
    kept, given = call(
        down_kernel,
        (jax.ShapeDtypeStruct(shape, F32), jax.ShapeDtypeStruct(shape, BF16)),
        0.1,
    )(partner, *weights, *started)
    sums = (kept + swap_cores(given).astype(F32)).astype(BF16).reshape(16, each, width)

    half = n_rows // 2
    prefill = sums[:, :half].reshape(16, 16, 4, width).transpose(1, 0, 2, 3).reshape(16, half, width)
    sums = exchange(jnp.concatenate([prefill, sums[:, half:]], axis=1), LZ)
    sums = sums.astype(F32).sum(0).astype(BF16)
    decode_out = lax.ppermute(
        sums[half:],
        ("x", "h", "l", "a", "b"),
        [
            (
                x * 64 + h * 16 + q * 4 + k * 2 + r,
                q * 64 + (h ^ 3 * k) * 16 + x * 4 + (h ^ r),
            )
            for x in range(4)
            for h in range(4)
            for q in range(4)
            for k in range(2)
            for r in range(2)
        ],
    )
    decode_out = call(decode_kernel, jax.ShapeDtypeStruct((rows // 2, steps, width), BF16), HINTS[4])(decode_out)
    decode_out = decode_out.transpose(1, 0, 2)
    mine = sums[:half].reshape(4, 2, 2, 4, width)
    theirs = lax.ppermute(mine[:, :, 1], "h", beside)
    prefill_out = call(prefill_kernel, jax.ShapeDtypeStruct((4, 16 * width), BF16), 0.1)(mine[:, :, 0], theirs)
    return prefill_out, decode_out


def solution(mesh):
    sizes = [size for _, size in SIZES]
    fine = Mesh(mesh.devices.reshape(sizes), [name for name, _ in SIZES])
    gx, yz = GX, ("l", "a", "b", "c")
    return jax.shard_map(
        local,
        mesh=fine,
        in_specs=(P(gx, yz), P(gx, yz), P(gx, yz), P(yz, gx), P(None, gx, None)),
        out_specs=(P(gx + yz, None), P(None, yz, gx)),
        check_vma=False,
    )
```

```python
import jax
import jax.numpy as jnp
from jax import lax
from jax.experimental import pallas as pl
from jax.experimental.pallas import tpu as pltpu
from jax.sharding import Mesh, PartitionSpec as P

BF16 = jnp.bfloat16
F32 = jnp.float32
SIZES = (("x", 4), ("h", 4), ("l", 2), ("a", 2), ("b", 4), ("c", 2))
GX = ("x", "h")
LZ = ("l", "a", "b")
UP = [(i, (i + 1) % 4) for i in range(4)]
DOWN = [(i, (i + 3) % 4) for i in range(4)]
VMEM = 10 * 2**20
HINTS = (4.95, 0.1, 1, 10, 5, 8, 5, 5)


def swap_cores(value):
    return lax.ppermute(value, "c", [(0, 1), (1, 0)])


def exchange(blocks, axes):
    return lax.all_to_all(blocks, axes, split_axis=0, concat_axis=0, tiled=True)


def near(value, axis):
    return lax.ppermute(value, axis, DOWN), lax.ppermute(value, axis, UP)


def far(following, previous, axis, hint):
    shape = previous.shape[:-2] + (previous.shape[-2] // 2, previous.shape[-1])
    halves = jax.ShapeDtypeStruct(shape, BF16)
    up, down = call(halves_kernel, (halves, halves), hint)(previous, following)
    return lax.ppermute(up, axis, UP), lax.ppermute(down, axis, DOWN)


def call(kernel, outs, hint, scratch=(), vmem=VMEM, **more):
    return pl.pallas_call(
        kernel,
        out_shape=outs,
        scratch_shapes=list(scratch),
        compiler_params=pltpu.CompilerParams(vmem_limit_bytes=vmem),
        cost_estimate=pl.CostEstimate(flops=int(hint * 1.1e9), bytes_accessed=2**20, transcendentals=0),
        **more,
    )


def dot(lhs, rhs):
    return jnp.dot(lhs, rhs, preferred_element_type=F32)


def weights_kernel(gate, up, out):
    ff = gate.shape[0]
    even = ff // 128 * 128
    out[:even] = gate[:even]
    out[even : 2 * even] = up[:even]
    out[2 * even : even + ff] = gate[even:]
    out[even + ff :] = up[even:]


def rows_kernel(tokens, decode, out):
    count = tokens.shape[0]
    to = lax.broadcasted_iota(jnp.int32, (count, count), 0)
    source = lax.broadcasted_iota(jnp.int32, (count, count), 1)
    half = count // 2
    place = to % half // 4 * 8 + to // half * 4 + to % 4
    moved = dot((place == source).astype(BF16), tokens[...])
    out[...] = jnp.concatenate([moved, decode[...].astype(F32)], axis=0).astype(BF16)


def halves_kernel(previous, following, up, down):
    half = up.shape[-2]
    up[...] = previous[..., :half, :]
    down[...] = following[..., half:, :]


def pair_kernel(own, opposite, out):
    out[0] = own[...]
    out[1] = opposite[...]


def half_product(feats, weights, which):
    x = lax.axis_index("x")
    own, following, first, second, previous = weights
    block = feats.shape[2]
    part = pl.ds(pl.multiple_of(which * block, block), block)
    opposite = jnp.concatenate([first[:, part], second[:, part]], axis=0)
    rhs = jnp.concatenate([own[:, part], following[:, part], opposite, previous[:, part]], axis=1)
    fill = jnp.zeros((-feats.shape[1] % 16, block), BF16)
    lhs = [
        jnp.concatenate(
            [part for b in range(4) for part in (feats[lax.rem(x + slot, 4) * 4 + b], fill)], axis=0
        )
        for slot in range(4)
    ]
    return lax.dot_general(
        jnp.concatenate(lhs, axis=1), rhs, (((1,), (1,)), ((), ())), preferred_element_type=F32
    )


def gate_up_start_kernel(feats, own, following, first, second, previous, out):
    out[...] = half_product(feats, (own, following, first, second, previous), lax.axis_index("c"))


def gate_up_kernel(feats, started, own, following, first, second, previous, partial, residue):
    h = lax.axis_index("h")
    blocks, rows, _ = partial.shape
    weights = (own, following, first, second, previous)
    total = started[...] + half_product(feats, weights, 1 - lax.axis_index("c"))
    stride = total.shape[0] // blocks
    for b in range(blocks):
        part = total[b * stride : b * stride + rows]
        rounded = part.astype(BF16)
        partial[b] = rounded

        @pl.when(b == h)
        def _():
            residue[...] = (part - rounded.astype(F32)).astype(BF16)


def hidden_kernel(parts, residue, out):
    ff = out.shape[1]
    sums = residue[...].astype(F32)
    for source in range(4):
        sums = sums + parts[source].astype(F32)
    even = ff // 128 * 128
    gate, up, tail = sums[:, :even], sums[:, even : 2 * even], sums[:, 2 * even :]
    out[:, :even] = (gate / (1.0 + jnp.exp(-gate)) * up).astype(BF16)
    gate, up = tail[:, : ff - even], tail[:, ff - even :]
    out[:, even:] = (gate / (1.0 + jnp.exp(-gate)) * up).astype(BF16)


def down_products(half, hidden, own, following, first, second, previous, store):
    x, core = lax.axis_index("x"), lax.axis_index("c")
    mine = hidden[pl.ds(pl.multiple_of(core * half, 16), half)]
    other = hidden[pl.ds(pl.multiple_of((1 - core) * half, 16), half)]
    decode = hidden[2 * half :].astype(F32)
    low, high = decode[:16].astype(BF16), decode[8:].astype(BF16)
    lhs = jnp.concatenate(
        [mine, jnp.where(core == 0, low, high), other, jnp.where(core == 0, high, low)], axis=0
    )
    for slot in range(4):
        for k in range(2):
            if slot == 2:
                weight = jnp.concatenate([first[k], second[k]], axis=0)
            else:
                weight = (own, following, None, previous)[slot][k]
            terms = dot(lhs, weight)
            store(lax.rem(x + slot, 4) * 2 + k, terms[: half + 16], terms[half + 16 :].astype(BF16))


def down_start_kernel(hidden, own, following, first, second, previous, kept, given):
    def store(at, mine, other):
        kept[at] = mine
        given[at] = other

    down_products(kept.shape[1] - 16, hidden, own, following, first, second, previous, store)


def down_kernel(hidden, own, following, first, second, previous, kept0, given0, kept, given):
    def store(at, mine, other):
        kept[at, 1] = mine
        given[at, 1] = other

    down_products(kept.shape[2] - 16, hidden, own, following, first, second, previous, store)
    kept[:, 0] = kept0[...]
    given[:, 0] = given0[...]


def prefill_kernel(mine, theirs, out):
    h = lax.axis_index("h")
    width = mine.shape[3]
    for q in range(mine.shape[0]):
        for k in range(mine.shape[1]):
            column = lax.bitwise_xor(h, 3 * k)
            for ref, at in ((mine, column), (theirs, lax.bitwise_xor(column, 1))):
                out[:, pl.ds(pl.multiple_of((q * 4 + at) * width, width), width)] = ref[q, k]


def decode_kernel(rows, out):
    core = lax.axis_index("c")
    count, steps, _ = out.shape
    wide = rows[...].astype(F32)
    skip = wide.shape[0] - count * steps
    for i in range(count):
        at = i * steps
        low, high = wide[at : at + steps], wide[skip + at : skip + at + steps]
        out[i] = jnp.where(core == 0, low, high).astype(BF16)


def local(tokens, gate_weight, up_weight, down_weight, decode_in):
    yz = lax.axis_index(("l", "a", "b", "c"))
    steps, rows, _ = decode_in.shape
    depth, ff = gate_weight.shape
    n_rows, block = tokens.shape
    n_dec = steps * rows
    width = down_weight.shape[1]
    each = -(-(n_rows + n_dec) // 32) * 16
    used, total = n_rows + n_dec, 2 * each

    decode_part = lax.dynamic_slice_in_dim(decode_in, yz * block, block, 2)
    feats = call(rows_kernel, jax.ShapeDtypeStruct((used, block), BF16), HINTS[7])(
        tokens, decode_part.transpose(1, 0, 2).reshape(n_dec, block)
    )
    feats = lax.ppermute(
        feats, ("h", "b"), [(h * 4 + b, b * 4 + h) for h in range(4) for b in range(4)]
    )
    feats = exchange(jnp.broadcast_to(feats, (16, used, block)), LZ)
    own = call(weights_kernel, jax.ShapeDtypeStruct((2 * ff, depth), BF16), 1)(
        gate_weight.T, up_weight.T
    )
    own_near = near(own, "x")
    own_far = far(*own_near, "x", HINTS[0])
    opposite = lax.ppermute(down_weight, "h", [(i, 3 - i) for i in range(4)])
    other = swap_cores(feats)

    weights = (own, own_near[0], *own_far, own_near[1])
    started = call(gate_up_start_kernel, jax.ShapeDtypeStruct((4 * total, 2 * ff), F32), HINTS[5])(feats, *weights)
    partial, residue = call(
        gate_up_kernel,
        (
            jax.ShapeDtypeStruct((4, used, 2 * ff), BF16),
            jax.ShapeDtypeStruct((used, 2 * ff), BF16),
        ),
        HINTS[1],
    )(other, started, *weights)
    parts = exchange(partial, "h")
    hidden = call(hidden_kernel, jax.ShapeDtypeStruct((used, ff), BF16), 1)(parts, residue)
    beside = [(0, 1), (1, 0), (2, 3), (3, 2)]
    partner = lax.ppermute(hidden, "h", beside)
    down = call(pair_kernel, jax.ShapeDtypeStruct((2, ff, width), BF16), HINTS[3])(down_weight, opposite)
    down_near = near(down, "x")
    down_far = far(*down_near, "x", HINTS[2])
    weights = (down, down_near[0], *down_far, down_near[1])
    shape = (8, each, width)
    started = call(
        down_start_kernel,
        (jax.ShapeDtypeStruct(shape, F32), jax.ShapeDtypeStruct(shape, BF16)),
        HINTS[6],
    )(hidden, *weights)
    started, partner = lax.optimization_barrier((started, partner))
    shape = (8, 2, each, width)
    kept, given = call(
        down_kernel,
        (jax.ShapeDtypeStruct(shape, F32), jax.ShapeDtypeStruct(shape, BF16)),
        0.1,
    )(partner, *weights, *started)
    sums = (kept + swap_cores(given).astype(F32)).astype(BF16).reshape(16, each, width)

    half = n_rows // 2
    prefill = sums[:, :half].reshape(16, 16, 4, width).transpose(1, 0, 2, 3).reshape(16, half, width)
    sums = exchange(jnp.concatenate([prefill, sums[:, half:]], axis=1), LZ)
    sums = sums.astype(F32).sum(0).astype(BF16)
    decode_out = lax.ppermute(
        sums[half:],
        ("x", "h", "l", "a", "b"),
        [
            (
                x * 64 + h * 16 + q * 4 + k * 2 + r,
                q * 64 + (h ^ 3 * k) * 16 + x * 4 + (h ^ r),
            )
            for x in range(4)
            for h in range(4)
            for q in range(4)
            for k in range(2)
            for r in range(2)
        ],
    )
    decode_out = call(decode_kernel, jax.ShapeDtypeStruct((rows // 2, steps, width), BF16), HINTS[4])(decode_out)
    decode_out = decode_out.transpose(1, 0, 2)
    mine = sums[:half].reshape(4, 2, 2, 4, width)
    theirs = lax.ppermute(mine[:, :, 1], "h", beside)
    prefill_out = call(prefill_kernel, jax.ShapeDtypeStruct((4, 16 * width), BF16), 0.1)(mine[:, :, 0], theirs)
    return prefill_out, decode_out


def solution(mesh):
    sizes = [size for _, size in SIZES]
    fine = Mesh(mesh.devices.reshape(sizes), [name for name, _ in SIZES])
    gx, yz = GX, ("l", "a", "b", "c")
    return jax.shard_map(
        local,
        mesh=fine,
        in_specs=(P(gx, yz), P(gx, yz), P(gx, yz), P(yz, gx), P(None, gx, None)),
        out_specs=(P(gx + yz, None), P(None, yz, gx)),
        check_vma=False,
    )
```
